128 devices in a mesh: dp: 16 (over y, z), expert: 8 (over x, core).
Axes of the slice: x: 4, y: 4, z: 4, core: 2. Of those that a mesh axis runs over, the one named last changes fastest.
Arguments:
- grad_out: bfloat16 [16384, 6144], P(('dp', 'expert')), may hold values from -6 to 6
- routes: int32 [16384, 2], P(('dp', 'expert')), may hold values from 0 to 31, all different within a row; in each aligned block of 128 rows (0 to 127, 128 to 255, ...) at most 9 rows name the same one
- loss_weight: int32 [16384], P(('dp', 'expert')), may hold values from 1 to 4
- saved_input: bfloat16 [32, 1152, 6144], P('dp', None, 'expert'), may hold values from -6 to 6
- saved_gate: bfloat16 [32, 1152, 1024], P('dp', None, 'expert'), may hold values from -8 to 8
- saved_up: bfloat16 [32, 1152, 1024], P('dp', None, 'expert'), may hold values from -6 to 6
- w_gate: bfloat16 [32, 6144, 1024], P('dp', 'expert'), may hold values from -0.1875 to 0.1875
- w_up: bfloat16 [32, 6144, 1024], P('dp', 'expert'), may hold values from -0.1875 to 0.1875
- w_down: bfloat16 [32, 1024, 6144], P('dp', None, 'expert'), may hold values from -0.078125 to 0.078125
Outputs:
- grad_input: bfloat16 [16384, 6144], P(('dp', 'expert'))
- grad_gate: bfloat16 [32, 6144, 1024], P('dp', 'expert')
- grad_up: bfloat16 [32, 6144, 1024], P('dp', 'expert')
- grad_down: bfloat16 [32, 1024, 6144], P('dp', None, 'expert')
The draws below stay inside these ranges and needn't reach their ends.
Inputs may be any that keep to these rules, and one draw needn't show every extreme that they name: `routes`: each row names two different experts; among the rows of one device no expert is named more than 9 times, and some device names some expert exactly 9 times.
All inputs are finite; a program needn't handle non-finite values.
Results may differ from the reference program's by a relative error of at most 0.0061.
Values may be sent and summed in bfloat16 or wider, within the bound.
No kernel may reach another device: no remote copies, remote signals or barrier semaphores. Data moves between devices by JAX's collectives and lax.ppermute only.
A program may use at most 192 MiB of HBM per device.

```python
import math
import jax
import jax.numpy as jnp
import numpy as np
from jax import lax

D = 6144
HW = 1024
TOK_DEV = 128
E = 32
CAP = 9
SLOTS = 1152
TOKENS = 16384
N_DP = 16
N_EXPERT = 8


def set_ends(entries, stream_key, least, largest):
    spot = [jax.random.randint(jax.random.fold_in(stream_key, axis), (), 0, length) for axis, length in enumerate(entries.shape)]
    widest = entries.shape.index(max(entries.shape))
    neighbour = spot[:widest] + [(spot[widest] + 1) % entries.shape[widest]] + spot[widest + 1:]
    return entries.at[tuple(spot)].set(least).at[tuple(neighbour)].set(largest)


def shard_levels(own_key, shape, cuts, low, high):
    factor_of = 1.0
    for dim, blocks in cuts:
        steps = jax.random.uniform(jax.random.fold_in(jax.random.fold_in(own_key, 6), dim), (blocks,), jnp.float32, low / len(cuts), high / len(cuts))
        factor_of = factor_of * jnp.repeat(jnp.exp(steps), shape[dim] // blocks).reshape((-1,) + (1,) * (len(shape) - 1 - dim))
    return factor_of


def deal_out(own_key, own, number, rows, amount, top, bound, slope):
    sequence = jax.random.permutation(own_key, amount)
    heavy_load, ordinary = shares(amount, rows * top, bound, slope, True), shares(amount, rows * top, bound, slope, False)
    places = jnp.arange(amount)

    def named(tallies, turn):
        used = int((tallies > 0).sum())
        fixed = max(1, used // 4)
        moved = fixed + (places - fixed + turn * (used - fixed)) % max(1, amount - fixed)
        return jnp.zeros((amount,), jnp.int32).at[sequence[jnp.where(places < fixed, places, moved)]].set(jnp.asarray(tallies, jnp.int32))

    tallies = jnp.where(number % 4 == 0, named(heavy_load, number // 4), named(ordinary, number - number // 4 - 1))
    mixed = jax.random.permutation(jax.random.fold_in(own, 3), amount)
    source_of, receiver = mixed[0:amount // 2 * 2:2], mixed[1:amount // 2 * 2:2]
    room = jnp.minimum(tallies[source_of] - 1, bound - tallies[receiver]) // 2
    room = jnp.where((source_of == sequence[0]) | (receiver == sequence[0]) | (tallies[receiver] == 0), 0, jnp.maximum(room, 0))
    moved = jax.random.randint(jax.random.fold_in(own, 4), (amount // 2,), 0, 1 << 20) % (room + 1)
    tallies = tallies.at[source_of].add(-moved).at[receiver].add(moved)
    labels = jnp.searchsorted(jnp.cumsum(tallies), jnp.arange(rows * top), side="right").astype(jnp.int32)
    grid = labels.reshape(top, rows).T
    grid = grid[jax.random.permutation(jax.random.fold_in(own, 1), rows)]
    turn = jax.random.randint(jax.random.fold_in(own, 2), (rows, 1), 0, top)
    return jnp.take_along_axis(grid, (jnp.arange(top)[None, :] + turn) % top, axis=1)


def shares(count, total, bound, lean, full):
    weights = [(1 << 20) // math.isqrt(standing ** lean) + 1 for standing in range(1, count + 1)]
    largest = bound if full else min(bound, max(-(-total // count), total * weights[0] // sum(weights)))
    least = 1 if total - largest >= count - 1 else 0
    counts, spare = [largest] + [least] * (count - 1), total - largest - least * (count - 1)
    while spare > 0:
        candidates = [i for i in range(1, count) if counts[i] < largest] or [i for i in range(1, count) if counts[i] < bound]
        pool, remaining = sum([weights[i] for i in candidates]), spare
        for i in candidates:
            addition = min(bound - counts[i], max(1, remaining * weights[i] // pool), spare)
            counts[i] = counts[i] + addition
            spare = spare - addition
    return np.array(counts)


def scatter_about(stream_key, dims, width, bound, pieces=(), kind=jnp.bfloat16):
    loudness = shard_levels(stream_key, dims, pieces, -0.22, 0.18) if pieces else 1.0
    result = jax.random.normal(stream_key, dims, jnp.float32) * width * loudness
    return jnp.minimum(jnp.maximum(result, -bound), bound).astype(kind)


def setup_inputs(seed: int = 0) -> dict:
    arg_keys = jax.random.split(jax.random.key(seed), 10)
    grad_out = scatter_about(arg_keys[0], (TOKENS, D), 1.0, 6.0, ((0, 128),))
    routes_keys = jax.random.split(jax.random.fold_in(arg_keys[1], 1), TOKENS // TOK_DEV)
    routes_turns = jax.random.permutation(jax.random.fold_in(arg_keys[1], 3), TOKENS // TOK_DEV)
    routes = jax.vmap(lambda own, number: deal_out(jax.random.fold_in(arg_keys[1], 2), own, number, TOK_DEV, E, 2, CAP, 1))(routes_keys, routes_turns).reshape((TOKENS, 2))
    loss_weight = set_ends(jax.random.randint(arg_keys[2], (TOKENS,), 1, 5), jax.random.fold_in(arg_keys[2], 1), 1, 4).astype(jnp.int32)
    saved_input = scatter_about(arg_keys[3], (E, SLOTS, D), 1.0, 6.0, ((0, 16), (2, 8)))
    saved_gate = scatter_about(arg_keys[4], (E, SLOTS, HW), 1.5, 8.0, ((0, 16), (2, 8)))
    saved_up = scatter_about(arg_keys[5], (E, SLOTS, HW), 1.0, 6.0, ((0, 16), (2, 8)))
    w_gate = scatter_about(arg_keys[6], (E, D, HW), HW ** -0.5, 0.1875, ((0, 16), (1, 8)))
    w_up = scatter_about(arg_keys[7], (E, D, HW), HW ** -0.5, 0.1875, ((0, 16), (1, 8)))
    w_down = scatter_about(arg_keys[8], (E, HW, D), D ** -0.5, 0.078125, ((0, 16), (2, 8)))
    return {"grad_out": grad_out, "routes": routes, "loss_weight": loss_weight, "saved_input": saved_input, "saved_gate": saved_gate, "saved_up": saved_up, "w_gate": w_gate, "w_up": w_up, "w_down": w_down}


def reference(grad_out, routes, loss_weight, saved_input, saved_gate, saved_up, w_gate, w_up, w_down):
    devices_all = N_DP * N_EXPERT
    highest = lax.Precision.HIGHEST
    flat_routes = routes.reshape(devices_all, TOK_DEV * 2)
    onehot = (flat_routes[:, :, None] == jnp.arange(E, dtype=jnp.int32)[None, None, :]).astype(jnp.int32)
    before = jnp.cumsum(onehot, axis=1) - onehot
    rank = jnp.sum(before * onehot, axis=2).astype(jnp.int32)
    device_ids = jnp.arange(devices_all, dtype=jnp.int32)[:, None]
    slot = device_ids * CAP + rank
    token_ids = device_ids * TOK_DEV + jnp.arange(TOK_DEV * 2, dtype=jnp.int32)[None, :] // 2
    where = (flat_routes * SLOTS + slot).reshape(-1).astype(jnp.int32)
    table = jnp.full((E * SLOTS,), TOKENS, jnp.int32).at[where].set(token_ids.reshape(-1).astype(jnp.int32))
    table = table.reshape(E, SLOTS)
    scaled = (grad_out.astype(jnp.float32) * loss_weight.astype(jnp.float32)[:, None] * 0.25).astype(jnp.bfloat16)
    padded = jnp.concatenate([scaled, jnp.zeros((1, D), jnp.bfloat16)], axis=0)

    def per_expert(carry, items):
        rows, inputs, gates, ups, gate_mat, up_mat, down_mat = items
        dispatched = padded[rows].astype(jnp.float32)
        dhidden = jnp.dot(dispatched, down_mat.astype(jnp.float32).T, precision=highest)
        gvals = gates.astype(jnp.float32)
        uvals = ups.astype(jnp.float32)
        sig = jax.nn.sigmoid(gvals)
        act = gvals * sig
        hidden = (act * uvals).astype(jnp.bfloat16).astype(jnp.float32)
        dgate = (dhidden * uvals * sig * (1.0 + gvals * (1.0 - sig))).astype(jnp.bfloat16).astype(jnp.float32)
        dup = (dhidden * act).astype(jnp.bfloat16).astype(jnp.float32)
        xvals = inputs.astype(jnp.float32)
        grad_d = jnp.dot(hidden.T, dispatched, precision=highest).astype(jnp.bfloat16)
        grad_g = jnp.dot(xvals.T, dgate, precision=highest).astype(jnp.bfloat16)
        grad_u = jnp.dot(xvals.T, dup, precision=highest).astype(jnp.bfloat16)
        slot_grad = jnp.dot(dgate, gate_mat.astype(jnp.float32).T, precision=highest)
        slot_grad = slot_grad + jnp.dot(dup, up_mat.astype(jnp.float32).T, precision=highest)
        slot_grad = slot_grad.astype(jnp.bfloat16).astype(jnp.float32)
        carry = carry.at[rows].add(slot_grad, mode="drop")
        return carry, (grad_g, grad_u, grad_d)

    start = jnp.zeros((TOKENS, D), jnp.float32)
    total, grads = lax.scan(per_expert, start, (table, saved_input, saved_gate, saved_up, w_gate, w_up, w_down))
    return total.astype(jnp.bfloat16), grads[0], grads[1], grads[2]
```

```python
import jax
import jax.numpy as jnp
from jax import lax
from jax.experimental import pallas as pl
from jax.experimental.pallas import tpu as pltpu
from jax.sharding import PartitionSpec as P

X_CHIPS = 4
VMEM = 48 * 2**20
CORES = 2
BF16 = jnp.bfloat16
F32 = jnp.float32


def pairs(dx, dc):
    return [
        (x * CORES + c, ((x + dx) % X_CHIPS) * CORES + (c + dc) % CORES)
        for x in range(X_CHIPS)
        for c in range(CORES)
    ]


def along_x(v, dx):
    return lax.ppermute(v, "expert", pairs(dx, 0))


def swap_core(v):
    return lax.ppermute(v, "expert", pairs(0, 1))


def dot(a, b, ca, cb):
    return lax.dot_general(a, b, (((ca,), (cb,)), ((), ())), preferred_element_type=F32)


def call(kernel, scalars, grid, in_specs, out_specs, out_shape, operands, scratch=()):
    return pl.pallas_call(
        kernel,
        grid_spec=pltpu.PrefetchScalarGridSpec(
            num_scalar_prefetch=1,
            grid=grid,
            in_specs=in_specs,
            out_specs=out_specs,
            scratch_shapes=scratch,
        ),
        out_shape=out_shape,
        compiler_params=pltpu.CompilerParams(vmem_limit_bytes=VMEM),
        cost_estimate=pl.CostEstimate(flops=1000, bytes_accessed=1000, transcendentals=0),
    )(scalars, *operands)


def out(shape, dtype):
    return jax.ShapeDtypeStruct(shape, dtype)


def unused(refs):
    return [pl.BlockSpec(memory_space=pl.ANY)] * len(refs)


def both_saved(where, gate, up, after):
    rows, lanes = gate.shape
    tile = rows // 2

    def kernel(where_ref, g_ref, u_ref, *refs):
        refs[-1][0] = g_ref[...]
        refs[-1][1] = u_ref[...]

    spec = pl.BlockSpec((tile, lanes), lambda i, s: (i, 0))
    return call(
        kernel,
        where,
        (2,),
        [spec, spec] + unused(after),
        pl.BlockSpec((2, tile, lanes), lambda i, s: (0, i, 0)),
        out((2, rows, lanes), gate.dtype),
        (gate, up, *after),
    )


def hidden_partials(where, e, dispatched, w_down, after):
    slots, cols = dispatched.shape
    units = w_down.shape[1]
    rows = slots // X_CHIPS
    block = rows // CORES
    tile = 256

    def kernel(where_ref, a_ref, w_ref, *refs):
        keep_ref, give_ref, acc_ref = refs[-3:]
        x, c = where_ref[0], where_ref[1]
        acc_ref[...] = dot(a_ref[...], w_ref[...], 1, 1)
        for i in range(X_CHIPS):
            base = (x + i) % X_CHIPS * rows
            keep_ref[i] = acc_ref[pl.ds(pl.multiple_of(base + c * block, block), block), :]
            give = acc_ref[pl.ds(pl.multiple_of(base + (1 - c) * block, block), block), :]
            give_ref[i] = give.astype(BF16)

    return call(
        kernel,
        where,
        (units // tile,),
        [
            pl.BlockSpec((slots, cols), lambda i, s: (0, 0)),
            pl.BlockSpec((None, tile, cols), lambda i, s: (e, i, 0)),
        ]
        + unused(after),
        [pl.BlockSpec((X_CHIPS, block, tile), lambda i, s: (0, 0, i))] * 2,
        [out((X_CHIPS, block, units), F32), out((X_CHIPS, block, units), BF16)],
        (dispatched, w_down, *after),
        [pltpu.VMEM((slots, tile), F32)],
    )


def pair_sums(where, keep, received, after):
    chips, block, units = keep.shape
    tile = 48

    def kernel(where_ref, k_ref, r_ref, *refs):
        outs = refs[-chips:]
        for i in range(chips):
            outs[i][...] = (k_ref[i] + r_ref[i].astype(F32)).astype(outs[i].dtype)

    return call(
        kernel,
        where,
        (block // tile,),
        [pl.BlockSpec((chips, tile, units), lambda i, s: (0, i, 0))] * 2 + unused(after),
        [pl.BlockSpec((tile, units), lambda i, s: (i, 0))] * chips,
        [out((block, units), F32 if i == 0 else BF16) for i in range(chips)],
        (keep, received, *after),
    )


def chip_sums(where, own, received, after):
    block, units = own.shape
    tile = 48
    count = len(received)

    def kernel(where_ref, o_ref, *refs):
        total = o_ref[...]
        for r in refs[:count]:
            total = total + r[...].astype(F32)
        refs[-1][...] = total.astype(BF16)

    spec = pl.BlockSpec((tile, units), lambda i, s: (i, 0))
    return call(
        kernel,
        where,
        (block // tile,),
        [spec] * (1 + count) + unused(after),
        spec,
        out((block, units), BF16),
        (own, *received, *after),
    )


def slot_gradient(where, e, pieces, saved, w_gate, w_up, after):
    count = len(pieces)
    block, units_all = pieces[0].shape
    flat = [r for v in saved for r in v]
    lanes = flat[0].shape[-1]
    slots = block * count
    cols = w_gate.shape[1]
    pair = CORES * block
    tile = 256

    def kernel(where_ref, *refs):
        piece_refs = refs[:count]
        saved_refs = refs[count : 3 * count]
        wg_ref, wu_ref = refs[3 * count : 3 * count + 2]
        dg_ref, du_ref, h_ref, sg_ref, dgs_ref, dus_ref = refs[-6:]
        k = pl.program_id(0)
        x, c = where_ref[0], where_ref[1]

        def fill(d_ref, core):
            at_rows = pl.ds(pl.multiple_of(core * block, block), block)
            own = (x - k + X_CHIPS) % X_CHIPS * pair + core * block
            all_rows = pl.ds(pl.multiple_of(own, block), block)
            for j in range(count):
                unit = (x - j % X_CHIPS + X_CHIPS) % X_CHIPS * CORES + (c if j < X_CHIPS else 1 - c)
                span = pl.ds(pl.multiple_of(unit * lanes, lanes), lanes)
                g = saved_refs[2 * j][at_rows, :].astype(F32)
                u = saved_refs[2 * j + 1][at_rows, :].astype(F32)
                part = d_ref[:, span].astype(F32)
                sig = 0.5 * jnp.tanh(0.5 * g) + 0.5
                act = g * sig
                h_ref[at_rows, span] = (act * u).astype(BF16)
                dg = (part * (u * sig * (1.0 + g * (1.0 - sig)))).astype(BF16)
                du = (part * act).astype(BF16)
                dg_ref[at_rows, span] = dg
                du_ref[at_rows, span] = du
                dgs_ref[all_rows, span] = dg
                dus_ref[all_rows, span] = du

        for i in range(X_CHIPS):

            @pl.when(k == i)
            def _(i=i):
                fill(piece_refs[i], c)
                fill(piece_refs[X_CHIPS + i], 1 - c)

        @pl.when(k >= X_CHIPS)
        def _():
            total = dot(dgs_ref[...], wg_ref[...], 1, 1) + dot(dus_ref[...], wu_ref[...], 1, 1)
            sg_ref[...] = total.astype(BF16)

    def rows(k, s):
        return (s[0] - jnp.minimum(k, X_CHIPS - 1) + X_CHIPS) % X_CHIPS

    def column(k):
        return jnp.maximum(k - X_CHIPS, 0)

    specs, operands = [], []
    for arrays in saved:
        for which, v in enumerate(arrays):
            if v.ndim == 3:
                specs.append(
                    pl.BlockSpec(
                        (None, pair, lanes),
                        lambda k, s, which=which: (which, e * X_CHIPS + rows(k, s), 0),
                    )
                )
            else:
                specs.append(pl.BlockSpec((pair, lanes), lambda k, s: (e * X_CHIPS + rows(k, s), 0)))
            operands.append(v)
    weight = pl.BlockSpec((None, tile, units_all), lambda k, s: (e, column(k), 0))
    return call(
        kernel,
        where,
        (X_CHIPS + cols // tile,),
        [pl.BlockSpec((block, units_all), lambda k, s: (0, 0))] * count + specs + [weight] * 2 + unused(after),
        [pl.BlockSpec((pair, units_all), lambda k, s: (rows(k, s), 0))] * 3
        + [pl.BlockSpec((slots, tile), lambda k, s: (0, column(k)))],
        [out((slots, units_all), BF16)] * 3 + [out((slots, cols), BF16)],
        (*pieces, *operands, w_gate, w_up, *after),
        [pltpu.VMEM((slots, units_all), BF16)] * 2,
    )


def down_gradient(where, h0, h1, d0, d1):
    slots, cols = d0.shape
    units = h0.shape[1]
    tile = 256

    def kernel(where_ref, h0_ref, h1_ref, d0_ref, d1_ref, o_ref):
        for e, (h_ref, d_ref) in enumerate(((h0_ref, d0_ref), (h1_ref, d1_ref))):

            @pl.when(pl.program_id(0) == e)
            def _(h_ref=h_ref, d_ref=d_ref):
                o_ref[...] = dot(h_ref[...], d_ref[...], 0, 0).astype(BF16)

    whole = pl.BlockSpec((slots, cols), lambda e, k, s: (0, 0))
    last = units // tile - 1
    return call(
        kernel,
        where,
        (2, units // tile),
        [
            pl.BlockSpec((slots, tile), lambda e, k, s: (0, jnp.where(e == 0, k, last))),
            pl.BlockSpec((slots, tile), lambda e, k, s: (0, jnp.where(e == 0, 0, k))),
            whole,
            whole,
        ],
        pl.BlockSpec((None, tile, cols), lambda e, k, s: (e, k, 0)),
        out((2, units, cols), BF16),
        (h0, h1, d0, d1),
    )


def up_gradients(where, saved_input, dg0, du0, dg1, du1):
    experts, slots, cols = saved_input.shape
    units = dg0.shape[1]
    tile = 256

    def kernel(where_ref, x_ref, dg0_ref, du0_ref, dg1_ref, du1_ref, og_ref, ou_ref):
        for e, (g_ref, u_ref) in enumerate(((dg0_ref, du0_ref), (dg1_ref, du1_ref))):
            @pl.when(pl.program_id(0) == e)
            def _(g_ref=g_ref, u_ref=u_ref):
                og_ref[...] = dot(x_ref[...], g_ref[...], 0, 0).astype(BF16)
                ou_ref[...] = dot(x_ref[...], u_ref[...], 0, 0).astype(BF16)

    whole = pl.BlockSpec((slots, units), lambda e, k, s: (0, 0))
    made = pl.BlockSpec((None, tile, units), lambda e, k, s: (e, k, 0))
    return call(
        kernel,
        where,
        (experts, cols // tile),
        [pl.BlockSpec((None, slots, tile), lambda e, k, s: (e, 0, k))] + [whole] * 4,
        [made, made],
        [out((experts, cols, units), BF16)] * 2,
        (saved_input, dg0, du0, dg1, du1),
    )


def body(grad_out, routes, loss_weight, saved_input, saved_gate, saved_up, w_gate, w_up, w_down):
    groups = lax.axis_size("dp")
    splits = lax.axis_size("expert")
    pos = lax.axis_index("expert")
    my_x, my_c = pos // CORES, pos % CORES
    where = jnp.stack([my_x, my_c]).astype(jnp.int32)
    experts = w_gate.shape[0]
    tokens = grad_out.shape[0]
    width = grad_out.shape[1]
    cols = width // splits
    slots = saved_input.shape[1]
    cap = slots // (groups * splits)
    lanes = saved_gate.shape[2]

    chosen = routes.reshape(-1)
    order = jnp.arange(chosen.shape[0], dtype=jnp.int32)
    same = (chosen[:, None] == chosen[None, :]) & (order[:, None] < order[None, :])
    rank = jnp.sum(same.astype(jnp.int32), axis=0)
    row = (chosen % experts) * slots + (chosen // experts) * (splits * cap) + pos * cap + rank
    row = row.reshape(tokens, 2).T
    code = jnp.concatenate([row // 64, row % 64], axis=0).astype(BF16)
    code = jnp.pad(code, ((0, 4), (0, cols - tokens)))
    code = jnp.concatenate([code, code], axis=1)

    scaled = (grad_out.astype(F32) * loss_weight.astype(F32)[:, None] * 0.25).astype(BF16)
    near, far = [], []
    for dx in range(X_CHIPS):
        piece = lax.dynamic_slice(
            scaled, (0, (my_x + dx) % X_CHIPS * (CORES * cols)), (tokens, CORES * cols)
        )
        piece = jnp.concatenate([piece, code], axis=0)
        if dx:
            piece = along_x(piece, dx)
        near.append(lax.dynamic_slice(piece, (0, my_c * cols), (tokens + 8, cols)))
        far.append(swap_core(lax.dynamic_slice(piece, (0, (1 - my_c) * cols), (tokens + 8, cols))))
    gathered = jnp.stack(near + far)
    codes = gathered[:, tokens : tokens + 4, :tokens].astype(jnp.int32)
    row_of = (codes[:, :2] * 64 + codes[:, 2:]).transpose(1, 0, 2).reshape(2, splits * tokens)
    gathered = gathered[:, :tokens].reshape(splits * tokens, cols)

    index = jnp.arange(slots, dtype=jnp.int32)[:, None]
    placed = [
        ((row_of[0][None, :] == index + e * slots) | (row_of[1][None, :] == index + e * slots)).astype(BF16)
        for e in range(experts)
    ]
    outgoing = [dot(placed[e], gathered, 1, 0).astype(BF16) for e in range(experts)]
    dispatched = [
        lax.all_to_all(
            o.reshape(groups, splits * cap, cols), "dp", split_axis=0, concat_axis=0, tiled=True
        ).reshape(slots, cols)
        for o in outgoing
    ]

    both = both_saved(
        where,
        saved_gate.reshape(experts * slots, lanes),
        saved_up.reshape(experts * slots, lanes),
        tuple(near),
    )
    ahead, behind = along_x(both, 1), along_x(both, 3)
    across = (along_x(ahead[0], 1), along_x(behind[1], 3))
    held = [(both, both), (ahead, ahead), across, (behind, behind)]
    both_o, ahead_o, behind_o = swap_core(both), swap_core(ahead), swap_core(behind)
    across_o = (swap_core(across[0]), swap_core(across[1]))
    held += [(both_o, both_o), (ahead_o, ahead_o), across_o, (behind_o, behind_o)]

    grads, hidden, back = [], [], []
    before_slot = ()
    before_partial, before_pair, before_sum = (both_o, ahead_o, behind_o, *across_o), (), ()
    for e in range(experts):
        keep, give = hidden_partials(where, e, dispatched[e], w_down, before_partial)
        own, *sent = pair_sums(where, keep, swap_core(give), before_pair)
        received = [along_x(v, dx) for dx, v in enumerate(sent, 1)]
        own = chip_sums(where, own, received, before_sum)
        pieces = [own] + [along_x(own, dx) for dx in range(1, X_CHIPS)]
        pieces = pieces + [swap_core(v) for v in pieces]
        dgate, dup, act, slot_grad = slot_gradient(where, e, pieces, held, w_gate, w_up, before_slot)
        before_partial, before_pair, before_sum = (own,), pieces[1:X_CHIPS], (slot_grad,)
        hidden.append(act)
        grads += [dgate, dup]
        returned = lax.all_to_all(
            slot_grad.reshape(groups, splits * cap, cols), "dp", split_axis=0, concat_axis=0, tiled=True
        )
        before_slot = (returned,)
        if e == experts - 1:
            grad_down = down_gradient(where, *hidden, *dispatched)
            grad_gate, grad_up = up_gradients(where, saved_input, *grads)
            returned, grad_down, grad_gate, grad_up = lax.optimization_barrier(
                (returned, grad_down, grad_gate, grad_up)
            )
        back.append(dot(placed[e], returned.reshape(slots, cols), 0, 0))

    combined = sum(back).astype(BF16).reshape(CORES, X_CHIPS, tokens, cols)
    mine, other = combined[0], swap_core(combined[1])
    grad_input = jnp.zeros((tokens, width), BF16)
    for dx in range(X_CHIPS):
        for core, v in ((my_c, mine), (1 - my_c, other)):
            piece = along_x(v[dx], X_CHIPS - dx) if dx else v[dx]
            at = ((my_x + dx) % X_CHIPS * CORES + core) * cols
            grad_input = lax.dynamic_update_slice(grad_input, piece, (0, at))
    return (grad_input, grad_gate, grad_up, grad_down)


def solution(mesh):
    return jax.shard_map(
        body,
        mesh=mesh,
        in_specs=(
            P(("dp", "expert"), None),
            P(("dp", "expert"), None),
            P(("dp", "expert")),
            P("dp", None, "expert"),
            P("dp", None, "expert"),
            P("dp", None, "expert"),
            P("dp", "expert", None),
            P("dp", "expert", None),
            P("dp", None, "expert"),
        ),
        out_specs=(
            P(("dp", "expert"), None),
            P("dp", "expert", None),
            P("dp", "expert", None),
            P("dp", None, "expert"),
        ),
        check_vma=False,
    )
```

```python
import jax
import jax.numpy as jnp
from jax import lax
from jax.experimental import pallas as pl
from jax.experimental.pallas import tpu as pltpu
from jax.sharding import PartitionSpec as P

X_CHIPS = 4
VMEM = 48 * 2**20
CORES = 2
BF16 = jnp.bfloat16
F32 = jnp.float32


def pairs(dx, dc):
    return [
        (x * CORES + c, ((x + dx) % X_CHIPS) * CORES + (c + dc) % CORES)
        for x in range(X_CHIPS)
        for c in range(CORES)
    ]


def along_x(v, dx):
    return lax.ppermute(v, "expert", pairs(dx, 0))


def swap_core(v):
    return lax.ppermute(v, "expert", pairs(0, 1))


def dot(a, b, ca, cb):
    return lax.dot_general(a, b, (((ca,), (cb,)), ((), ())), preferred_element_type=F32)


def call(kernel, scalars, grid, in_specs, out_specs, out_shape, operands, scratch=(), cost=1000):
    return pl.pallas_call(
        kernel,
        grid_spec=pltpu.PrefetchScalarGridSpec(
            num_scalar_prefetch=1,
            grid=grid,
            in_specs=in_specs,
            out_specs=out_specs,
            scratch_shapes=scratch,
        ),
        out_shape=out_shape,
        compiler_params=pltpu.CompilerParams(vmem_limit_bytes=VMEM),
        cost_estimate=pl.CostEstimate(flops=1000, bytes_accessed=cost, transcendentals=0),
    )(scalars, *operands)


def out(shape, dtype):
    return jax.ShapeDtypeStruct(shape, dtype)


def unused(refs):
    return [pl.BlockSpec(memory_space=pl.ANY)] * len(refs)


def both_saved(where, gate, up, after):
    rows, lanes = gate.shape
    tile = rows // 2

    def kernel(where_ref, g_ref, u_ref, *refs):
        refs[-1][0] = g_ref[...]
        refs[-1][1] = u_ref[...]

    spec = pl.BlockSpec((tile, lanes), lambda i, s: (i, 0))
    return call(
        kernel,
        where,
        (2,),
        [spec, spec] + unused(after),
        pl.BlockSpec((2, tile, lanes), lambda i, s: (0, i, 0)),
        out((2, rows, lanes), gate.dtype),
        (gate, up, *after),
    )


def forwarded(where, ahead, behind, after):
    _, rows, lanes = ahead.shape
    tile = rows // 2

    def kernel(where_ref, a_ref, b_ref, *refs):
        refs[-2][...] = a_ref[...]
        refs[-1][...] = b_ref[...]

    made = pl.BlockSpec((tile, lanes), lambda i, s: (i, 0))
    return call(
        kernel,
        where,
        (2,),
        [
            pl.BlockSpec((None, tile, lanes), lambda i, s: (0, i, 0)),
            pl.BlockSpec((None, tile, lanes), lambda i, s: (1, i, 0)),
        ]
        + unused(after),
        [made, made],
        [out((rows, lanes), ahead.dtype)] * 2,
        (ahead, behind, *after),
    )


def hidden_partials(where, e, dispatched, w_down, after):
    slots, cols = dispatched.shape
    units = w_down.shape[1]
    rows = slots // X_CHIPS
    block = rows // CORES
    tile = 256

    def kernel(where_ref, a_ref, w_ref, *refs):
        keep_ref, give_ref, acc_ref = refs[-3:]
        x, c = where_ref[0], where_ref[1]
        acc_ref[...] = dot(a_ref[...], w_ref[...], 1, 1)
        for i in range(X_CHIPS):
            base = (x + i) % X_CHIPS * rows
            keep_ref[i] = acc_ref[pl.ds(pl.multiple_of(base + c * block, block), block), :]
            give = acc_ref[pl.ds(pl.multiple_of(base + (1 - c) * block, block), block), :]
            give_ref[i] = give.astype(BF16)

    return call(
        kernel,
        where,
        (units // tile,),
        [
            pl.BlockSpec((slots, cols), lambda i, s: (0, 0)),
            pl.BlockSpec((None, tile, cols), lambda i, s: (e, i, 0)),
        ]
        + unused(after),
        [pl.BlockSpec((X_CHIPS, block, tile), lambda i, s: (0, 0, i))] * 2,
        [out((X_CHIPS, block, units), F32), out((X_CHIPS, block, units), BF16)],
        (dispatched, w_down, *after),
        [pltpu.VMEM((slots, tile), F32)],
    )


def pair_sums(where, keep, received, after):
    chips, block, units = keep.shape
    tile = 48

    def kernel(where_ref, k_ref, r_ref, *refs):
        outs = refs[-chips:]
        for i in range(chips):
            outs[i][...] = (k_ref[i] + r_ref[i].astype(F32)).astype(outs[i].dtype)

    return call(
        kernel,
        where,
        (block // tile,),
        [pl.BlockSpec((chips, tile, units), lambda i, s: (0, i, 0))] * 2 + unused(after),
        [pl.BlockSpec((tile, units), lambda i, s: (i, 0))] * chips,
        [out((block, units), F32 if i == 0 else BF16) for i in range(chips)],
        (keep, received, *after),
    )


def chip_sums(where, own, received, after):
    block, units = own.shape
    tile = 48
    count = len(received)

    def kernel(where_ref, o_ref, *refs):
        total = o_ref[...]
        for r in refs[:count]:
            total = total + r[...].astype(F32)
        refs[-1][...] = total.astype(BF16)

    spec = pl.BlockSpec((tile, units), lambda i, s: (i, 0))
    return call(
        kernel,
        where,
        (block // tile,),
        [spec] * (1 + count) + unused(after),
        spec,
        out((block, units), BF16),
        (own, *received, *after),
    )


def slot_gradient(where, e, pieces, saved, w_gate, w_up, after):
    count = len(pieces)
    block, units_all = pieces[0].shape
    flat = [r for v in saved for r in v]
    lanes = flat[0].shape[-1]
    slots = block * count
    cols = w_gate.shape[1]
    pair = CORES * block
    tile = 256
    chunk = 48

    def kernel(where_ref, *refs):
        piece_refs = refs[:count]
        saved_refs = refs[count : 3 * count]
        wg_ref, wu_ref = refs[3 * count : 3 * count + 2]
        dg_ref, du_ref, h_ref, sg_ref, dgs_ref, dus_ref, part_ref = refs[-7:]
        k = pl.program_id(0)
        x, c = where_ref[0], where_ref[1]

        for i in range(X_CHIPS):

            @pl.when(k == i)
            def _(i=i):
                for near, core in ((True, c), (False, 1 - c)):
                    rows_here = pl.ds(pl.multiple_of(core * block, block), block)
                    part_ref[rows_here, :] = piece_refs[i if near else X_CHIPS + i][...]

        @pl.when(k < X_CHIPS)
        def _():
            base = (x - k + X_CHIPS) % X_CHIPS * pair

            @pl.loop(0, pair // chunk)
            def _(r):
                here = pl.ds(pl.multiple_of(r * chunk, chunk), chunk)
                whole = pl.ds(pl.multiple_of(base + r * chunk, chunk), chunk)
                for j in range(count):
                    unit = (x - j % X_CHIPS + X_CHIPS) % X_CHIPS * CORES + (c if j < X_CHIPS else 1 - c)
                    span = pl.ds(pl.multiple_of(unit * lanes, lanes), lanes)
                    g = saved_refs[2 * j][here, :].astype(F32)
                    u = saved_refs[2 * j + 1][here, :].astype(F32)
                    part = part_ref[here, span].astype(F32)
                    sig = 0.5 * jnp.tanh(0.5 * g) + 0.5
                    act = g * sig
                    h_ref[here, span] = (act * u).astype(BF16)
                    dg = (part * (u * sig * (1.0 + g * (1.0 - sig)))).astype(BF16)
                    du = (part * act).astype(BF16)
                    dg_ref[here, span] = dg
                    du_ref[here, span] = du
                    dgs_ref[whole, span] = dg
                    dus_ref[whole, span] = du

        @pl.when(k >= X_CHIPS)
        def _():
            total = dot(dgs_ref[...], wg_ref[...], 1, 1) + dot(dus_ref[...], wu_ref[...], 1, 1)
            sg_ref[...] = total.astype(BF16)

    def rows(k, s):
        return (s[0] - jnp.minimum(k, X_CHIPS - 1) + X_CHIPS) % X_CHIPS

    def column(k):
        return jnp.maximum(k - X_CHIPS, 0)

    specs, operands = [], []
    for arrays in saved:
        for which, v in enumerate(arrays):
            if v.ndim == 3:
                specs.append(
                    pl.BlockSpec(
                        (None, pair, lanes),
                        lambda k, s, which=which: (which, e * X_CHIPS + rows(k, s), 0),
                    )
                )
            else:
                specs.append(pl.BlockSpec((pair, lanes), lambda k, s: (e * X_CHIPS + rows(k, s), 0)))
            operands.append(v)
    weight = pl.BlockSpec((None, tile, units_all), lambda k, s: (e, column(k), 0))
    return call(
        kernel,
        where,
        (X_CHIPS + cols // tile,),
        [pl.BlockSpec((block, units_all), lambda k, s: (0, 0))] * count + specs + [weight] * 2 + unused(after),
        [pl.BlockSpec((pair, units_all), lambda k, s: (rows(k, s), 0))] * 3
        + [pl.BlockSpec((slots, tile), lambda k, s: (0, column(k)))],
        [out((slots, units_all), BF16)] * 3 + [out((slots, cols), BF16)],
        (*pieces, *operands, w_gate, w_up, *after),
        [pltpu.VMEM((slots, units_all), BF16)] * 2 + [pltpu.VMEM((pair, units_all), BF16)],
        50_000_000,
    )


def down_gradient(where, h0, h1, d0, d1):
    slots, cols = d0.shape
    units = h0.shape[1]
    tile = 256

    def kernel(where_ref, h0_ref, h1_ref, d0_ref, d1_ref, o_ref):
        for e, (h_ref, d_ref) in enumerate(((h0_ref, d0_ref), (h1_ref, d1_ref))):

            @pl.when(pl.program_id(0) == e)
            def _(h_ref=h_ref, d_ref=d_ref):
                o_ref[...] = dot(h_ref[...], d_ref[...], 0, 0).astype(BF16)

    whole = pl.BlockSpec((slots, cols), lambda e, k, s: (0, 0))
    last = units // tile - 1
    return call(
        kernel,
        where,
        (2, units // tile),
        [
            pl.BlockSpec((slots, tile), lambda e, k, s: (0, jnp.where(e == 0, k, last))),
            pl.BlockSpec((slots, tile), lambda e, k, s: (0, jnp.where(e == 0, 0, k))),
            whole,
            whole,
        ],
        pl.BlockSpec((None, tile, cols), lambda e, k, s: (e, k, 0)),
        out((2, units, cols), BF16),
        (h0, h1, d0, d1),
    )


def up_gradients(where, saved_input, dg0, du0, dg1, du1, after):
    experts, slots, cols = saved_input.shape
    units = dg0.shape[1]
    tile = 256

    def kernel(where_ref, x_ref, dg0_ref, du0_ref, dg1_ref, du1_ref, *refs):
        og_ref, ou_ref = refs[-2:]
        for e, (g_ref, u_ref) in enumerate(((dg0_ref, du0_ref), (dg1_ref, du1_ref))):
            @pl.when(pl.program_id(0) == e)
            def _(g_ref=g_ref, u_ref=u_ref):
                og_ref[...] = dot(x_ref[...], g_ref[...], 0, 0).astype(BF16)
                ou_ref[...] = dot(x_ref[...], u_ref[...], 0, 0).astype(BF16)

    whole = pl.BlockSpec((slots, units), lambda e, k, s: (0, 0))
    made = pl.BlockSpec((None, tile, units), lambda e, k, s: (e, k, 0))
    return call(
        kernel,
        where,
        (experts, cols // tile),
        [pl.BlockSpec((None, slots, tile), lambda e, k, s: (e, 0, k))] + [whole] * 4 + unused(after),
        [made, made],
        [out((experts, cols, units), BF16)] * 2,
        (saved_input, dg0, du0, dg1, du1, *after),
    )


def body(grad_out, routes, loss_weight, saved_input, saved_gate, saved_up, w_gate, w_up, w_down):
    groups = lax.axis_size("dp")
    splits = lax.axis_size("expert")
    pos = lax.axis_index("expert")
    my_x, my_c = pos // CORES, pos % CORES
    where = jnp.stack([my_x, my_c]).astype(jnp.int32)
    experts = w_gate.shape[0]
    tokens = grad_out.shape[0]
    width = grad_out.shape[1]
    cols = width // splits
    slots = saved_input.shape[1]
    cap = slots // (groups * splits)
    lanes = saved_gate.shape[2]

    chosen = routes.reshape(-1)
    order = jnp.arange(chosen.shape[0], dtype=jnp.int32)
    same = (chosen[:, None] == chosen[None, :]) & (order[:, None] < order[None, :])
    rank = jnp.sum(same.astype(jnp.int32), axis=0)
    row = (chosen % experts) * slots + (chosen // experts) * (splits * cap) + pos * cap + rank
    row = row.reshape(tokens, 2).T
    code = jnp.concatenate([row // 64, row % 64], axis=0).astype(BF16)
    code = jnp.pad(code, ((0, 4), (0, cols - tokens)))
    code = jnp.concatenate([code, code], axis=1)

    scaled = (grad_out.astype(F32) * loss_weight.astype(F32)[:, None] * 0.25).astype(BF16)
    near, far = [], []
    for dx in range(X_CHIPS):
        piece = lax.dynamic_slice(
            scaled, (0, (my_x + dx) % X_CHIPS * (CORES * cols)), (tokens, CORES * cols)
        )
        piece = jnp.concatenate([piece, code], axis=0)
        if dx:
            piece = along_x(piece, dx)
        near.append(lax.dynamic_slice(piece, (0, my_c * cols), (tokens + 8, cols)))
        far.append(swap_core(lax.dynamic_slice(piece, (0, (1 - my_c) * cols), (tokens + 8, cols))))
    gathered = jnp.stack(near + far)
    codes = gathered[:, tokens : tokens + 4, :tokens].astype(jnp.int32)
    row_of = (codes[:, :2] * 64 + codes[:, 2:]).transpose(1, 0, 2).reshape(2, splits * tokens)
    gathered = gathered[:, :tokens].reshape(splits * tokens, cols)

    index = jnp.arange(slots, dtype=jnp.int32)[:, None]
    placed = [
        ((row_of[0][None, :] == index + e * slots) | (row_of[1][None, :] == index + e * slots)).astype(BF16)
        for e in range(experts)
    ]
    outgoing = [dot(placed[e], gathered, 1, 0).astype(BF16) for e in range(experts)]
    dispatched = [
        lax.all_to_all(
            o.reshape(groups, splits * cap, cols), "dp", split_axis=0, concat_axis=0, tiled=True
        ).reshape(slots, cols)
        for o in outgoing
    ]

    both = both_saved(
        where,
        saved_gate.reshape(experts * slots, lanes),
        saved_up.reshape(experts * slots, lanes),
        (gathered,),
    )
    ahead, behind = along_x(both, 1), along_x(both, 3)
    pick_a, pick_b = forwarded(where, ahead, behind, ())
    across = (along_x(pick_a, 1), along_x(pick_b, 3))
    held = [(both, both), (ahead, ahead), across, (behind, behind)]
    both_o, ahead_o, behind_o = swap_core(both), swap_core(ahead), swap_core(behind)
    across_o = (swap_core(across[0]), swap_core(across[1]))
    held += [(both_o, both_o), (ahead_o, ahead_o), across_o, (behind_o, behind_o)]

    def partials(e, after, after_pair):
        keep, give = hidden_partials(where, e, dispatched[e], w_down, after)
        return pair_sums(where, keep, swap_core(give), after_pair)

    def exchanged(sent):
        return [along_x(v, dx) for dx, v in enumerate(sent, 1)]

    def spread(own):
        pieces = [own] + [along_x(own, dx) for dx in range(1, X_CHIPS)]
        return pieces + [swap_core(v) for v in pieces]

    def give_back(slot_grad):
        returned = lax.all_to_all(
            slot_grad.reshape(groups, splits * cap, cols), "dp", split_axis=0, concat_axis=0, tiled=True
        )
        return returned.reshape(slots, cols)

    first0, *sent0 = partials(0, (both_o, ahead_o, behind_o, *across), ())
    own0 = chip_sums(where, first0, exchanged(sent0), across_o)
    pieces0 = spread(own0)
    first1, *sent1 = partials(1, (own0,), ())
    own1 = chip_sums(where, first1, exchanged(sent1), ())
    dgate0, dup0, hidden0, slot_grad0 = slot_gradient(where, 0, pieces0, held, w_gate, w_up, (own1,))
    returned0 = give_back(slot_grad0)
    pieces1 = spread(own1)
    dgate1, dup1, hidden1, slot_grad1 = slot_gradient(where, 1, pieces1, held, w_gate, w_up, ())
    returned1 = give_back(slot_grad1)
    back0 = dot(placed[0], returned0, 0, 0)
    grad_down = down_gradient(where, hidden0, hidden1, *dispatched)
    grad_gate, grad_up = up_gradients(where, saved_input, dgate0, dup0, dgate1, dup1, (back0,))
    returned1, grad_down, grad_gate, grad_up = lax.optimization_barrier(
        (returned1, grad_down, grad_gate, grad_up)
    )
    back = [back0, dot(placed[1], returned1, 0, 0)]

    combined = sum(back).astype(BF16).reshape(CORES, X_CHIPS, tokens, cols)
    mine, other = combined[0], swap_core(combined[1])
    grad_input = jnp.zeros((tokens, width), BF16)
    for dx in range(X_CHIPS):
        for core, v in ((my_c, mine), (1 - my_c, other)):
            piece = along_x(v[dx], X_CHIPS - dx) if dx else v[dx]
            at = ((my_x + dx) % X_CHIPS * CORES + core) * cols
            grad_input = lax.dynamic_update_slice(grad_input, piece, (0, at))
    return (grad_input, grad_gate, grad_up, grad_down)


def solution(mesh):
    return jax.shard_map(
        body,
        mesh=mesh,
        in_specs=(
            P(("dp", "expert"), None),
            P(("dp", "expert"), None),
            P(("dp", "expert")),
            P("dp", None, "expert"),
            P("dp", None, "expert"),
            P("dp", None, "expert"),
            P("dp", "expert", None),
            P("dp", "expert", None),
            P("dp", None, "expert"),
        ),
        out_specs=(
            P(("dp", "expert"), None),
            P("dp", "expert", None),
            P("dp", "expert", None),
            P("dp", None, "expert"),
        ),
        check_vma=False,
    )
```

```python
import jax
import jax.numpy as jnp
from jax import lax
from jax.experimental import pallas as pl
from jax.experimental.pallas import tpu as pltpu
from jax.sharding import PartitionSpec as P

X_CHIPS = 4
VMEM = 48 * 2**20
CORES = 2
BF16 = jnp.bfloat16
F32 = jnp.float32


def pairs(dx, dc):
    return [
        (x * CORES + c, ((x + dx) % X_CHIPS) * CORES + (c + dc) % CORES)
        for x in range(X_CHIPS)
        for c in range(CORES)
    ]


def along_x(v, dx):
    return lax.ppermute(v, "expert", pairs(dx, 0))


def swap_core(v):
    return lax.ppermute(v, "expert", pairs(0, 1))


def dot(a, b, ca, cb):
    return lax.dot_general(a, b, (((ca,), (cb,)), ((), ())), preferred_element_type=F32)


def call(kernel, scalars, grid, in_specs, out_specs, out_shape, operands, scratch=(), cost=1000):
    return pl.pallas_call(
        kernel,
        grid_spec=pltpu.PrefetchScalarGridSpec(
            num_scalar_prefetch=1,
            grid=grid,
            in_specs=in_specs,
            out_specs=out_specs,
            scratch_shapes=scratch,
        ),
        out_shape=out_shape,
        compiler_params=pltpu.CompilerParams(vmem_limit_bytes=VMEM),
        cost_estimate=pl.CostEstimate(flops=1000, bytes_accessed=cost, transcendentals=0),
    )(scalars, *operands)


def out(shape, dtype):
    return jax.ShapeDtypeStruct(shape, dtype)


def unused(refs):
    return [pl.BlockSpec(memory_space=pl.ANY)] * len(refs)


def both_saved(where, gate, up, after):
    rows, lanes = gate.shape
    tile = rows // 2

    def kernel(where_ref, g_ref, u_ref, *refs):
        refs[-1][0] = g_ref[...]
        refs[-1][1] = u_ref[...]

    spec = pl.BlockSpec((tile, lanes), lambda i, s: (i, 0))
    return call(
        kernel,
        where,
        (2,),
        [spec, spec] + unused(after),
        pl.BlockSpec((2, tile, lanes), lambda i, s: (0, i, 0)),
        out((2, rows, lanes), gate.dtype),
        (gate, up, *after),
    )


def forwarded(where, ahead, behind, after):
    _, rows, lanes = ahead.shape
    tile = rows // 2

    def kernel(where_ref, a_ref, b_ref, *refs):
        refs[-2][...] = a_ref[...]
        refs[-1][...] = b_ref[...]

    made = pl.BlockSpec((tile, lanes), lambda i, s: (i, 0))
    return call(
        kernel,
        where,
        (2,),
        [
            pl.BlockSpec((None, tile, lanes), lambda i, s: (0, i, 0)),
            pl.BlockSpec((None, tile, lanes), lambda i, s: (1, i, 0)),
        ]
        + unused(after),
        [made, made],
        [out((rows, lanes), ahead.dtype)] * 2,
        (ahead, behind, *after),
    )


def hidden_partials(where, e, dispatched, w_down, after):
    slots, cols = dispatched.shape
    units = w_down.shape[1]
    rows = slots // X_CHIPS
    block = rows // CORES
    tile = 256

    def kernel(where_ref, a_ref, w_ref, *refs):
        keep_ref, give_ref, acc_ref = refs[-3:]
        x, c = where_ref[0], where_ref[1]
        acc_ref[...] = dot(a_ref[...], w_ref[...], 1, 1)
        for i in range(X_CHIPS):
            base = (x + i) % X_CHIPS * rows
            keep_ref[i] = acc_ref[pl.ds(pl.multiple_of(base + c * block, block), block), :]
            give = acc_ref[pl.ds(pl.multiple_of(base + (1 - c) * block, block), block), :]
            give_ref[i] = give.astype(BF16)

    return call(
        kernel,
        where,
        (units // tile,),
        [
            pl.BlockSpec((slots, cols), lambda i, s: (0, 0)),
            pl.BlockSpec((None, tile, cols), lambda i, s: (e, i, 0)),
        ]
        + unused(after),
        [pl.BlockSpec((X_CHIPS, block, tile), lambda i, s: (0, 0, i))] * 2,
        [out((X_CHIPS, block, units), F32), out((X_CHIPS, block, units), BF16)],
        (dispatched, w_down, *after),
        [pltpu.VMEM((slots, tile), F32)],
    )


def pair_sums(where, keep, received, after):
    chips, block, units = keep.shape
    tile = 48

    def kernel(where_ref, k_ref, r_ref, *refs):
        outs = refs[-chips:]
        for i in range(chips):
            outs[i][...] = (k_ref[i] + r_ref[i].astype(F32)).astype(outs[i].dtype)

    return call(
        kernel,
        where,
        (block // tile,),
        [pl.BlockSpec((chips, tile, units), lambda i, s: (0, i, 0))] * 2 + unused(after),
        [pl.BlockSpec((tile, units), lambda i, s: (i, 0))] * chips,
        [out((block, units), F32 if i == 0 else BF16) for i in range(chips)],
        (keep, received, *after),
    )


def chip_sums(where, own, received, after):
    block, units = own.shape
    tile = 48
    count = len(received)

    def kernel(where_ref, o_ref, *refs):
        total = o_ref[...]
        for r in refs[:count]:
            total = total + r[...].astype(F32)
        refs[-1][...] = total.astype(BF16)

    spec = pl.BlockSpec((tile, units), lambda i, s: (i, 0))
    return call(
        kernel,
        where,
        (block // tile,),
        [spec] * (1 + count) + unused(after),
        spec,
        out((block, units), BF16),
        (own, *received, *after),
    )


def slot_gradient(where, e, pieces, saved, w_gate, w_up, after):
    count = len(pieces)
    block, units_all = pieces[0].shape
    flat = [r for v in saved for r in v]
    lanes = flat[0].shape[-1]
    slots = block * count
    cols = w_gate.shape[1]
    pair = CORES * block
    tile = 256
    chunk = 48

    def kernel(where_ref, *refs):
        piece_refs = refs[:count]
        saved_refs = refs[count : 3 * count]
        wg_ref, wu_ref = refs[3 * count : 3 * count + 2]
        dg_ref, du_ref, h_ref, sg_ref, dgs_ref, dus_ref, part_ref = refs[-7:]
        k = pl.program_id(0)
        x, c = where_ref[0], where_ref[1]

        for i in range(X_CHIPS):

            @pl.when(k == i)
            def _(i=i):
                for near, core in ((True, c), (False, 1 - c)):
                    rows_here = pl.ds(pl.multiple_of(core * block, block), block)
                    part_ref[rows_here, :] = piece_refs[i if near else X_CHIPS + i][...]

        @pl.when(k < X_CHIPS)
        def _():
            base = (x - k + X_CHIPS) % X_CHIPS * pair

            @pl.loop(0, pair // chunk)
            def _(r):
                here = pl.ds(pl.multiple_of(r * chunk, chunk), chunk)
                whole = pl.ds(pl.multiple_of(base + r * chunk, chunk), chunk)
                for j in range(count):
                    unit = (x - j % X_CHIPS + X_CHIPS) % X_CHIPS * CORES + (c if j < X_CHIPS else 1 - c)
                    span = pl.ds(pl.multiple_of(unit * lanes, lanes), lanes)
                    g = saved_refs[2 * j][here, :].astype(F32)
                    u = saved_refs[2 * j + 1][here, :].astype(F32)
                    part = part_ref[here, span].astype(F32)
                    sig = 0.5 * jnp.tanh(0.5 * g) + 0.5
                    act = g * sig
                    h_ref[here, span] = (act * u).astype(BF16)
                    dg = (part * (u * sig * (1.0 + g * (1.0 - sig)))).astype(BF16)
                    du = (part * act).astype(BF16)
                    dg_ref[here, span] = dg
                    du_ref[here, span] = du
                    dgs_ref[whole, span] = dg
                    dus_ref[whole, span] = du

        @pl.when(k >= X_CHIPS)
        def _():
            total = dot(dgs_ref[...], wg_ref[...], 1, 1) + dot(dus_ref[...], wu_ref[...], 1, 1)
            sg_ref[...] = total.astype(BF16)

    def rows(k, s):
        return (s[0] - jnp.minimum(k, X_CHIPS - 1) + X_CHIPS) % X_CHIPS

    def column(k):
        return jnp.maximum(k - X_CHIPS, 0)

    specs, operands = [], []
    for arrays in saved:
        for which, v in enumerate(arrays):
            if v.ndim == 3:
                specs.append(
                    pl.BlockSpec(
                        (None, pair, lanes),
                        lambda k, s, which=which: (which, e * X_CHIPS + rows(k, s), 0),
                    )
                )
            else:
                specs.append(pl.BlockSpec((pair, lanes), lambda k, s: (e * X_CHIPS + rows(k, s), 0)))
            operands.append(v)
    weight = pl.BlockSpec((None, tile, units_all), lambda k, s: (e, column(k), 0))
    return call(
        kernel,
        where,
        (X_CHIPS + cols // tile,),
        [pl.BlockSpec((block, units_all), lambda k, s: (0, 0))] * count + specs + [weight] * 2 + unused(after),
        [pl.BlockSpec((pair, units_all), lambda k, s: (rows(k, s), 0))] * 3
        + [pl.BlockSpec((slots, tile), lambda k, s: (0, column(k)))],
        [out((slots, units_all), BF16)] * 3 + [out((slots, cols), BF16)],
        (*pieces, *operands, w_gate, w_up, *after),
        [pltpu.VMEM((slots, units_all), BF16)] * 2 + [pltpu.VMEM((pair, units_all), BF16)],
        50_000_000,
    )


def down_gradient(where, h0, h1, d0, d1):
    slots, cols = d0.shape
    units = h0.shape[1]
    tile = 256

    def kernel(where_ref, h0_ref, h1_ref, d0_ref, d1_ref, o_ref):
        for e, (h_ref, d_ref) in enumerate(((h0_ref, d0_ref), (h1_ref, d1_ref))):

            @pl.when(pl.program_id(0) == e)
            def _(h_ref=h_ref, d_ref=d_ref):
                o_ref[...] = dot(h_ref[...], d_ref[...], 0, 0).astype(BF16)

    whole = pl.BlockSpec((slots, cols), lambda e, k, s: (0, 0))
    last = units // tile - 1
    return call(
        kernel,
        where,
        (2, units // tile),
        [
            pl.BlockSpec((slots, tile), lambda e, k, s: (0, jnp.where(e == 0, k, last))),
            pl.BlockSpec((slots, tile), lambda e, k, s: (0, jnp.where(e == 0, 0, k))),
            whole,
            whole,
        ],
        pl.BlockSpec((None, tile, cols), lambda e, k, s: (e, k, 0)),
        out((2, units, cols), BF16),
        (h0, h1, d0, d1),
    )


def up_gradients(where, saved_input, dg0, du0, dg1, du1, after):
    experts, slots, cols = saved_input.shape
    units = dg0.shape[1]
    tile = 256

    def kernel(where_ref, x_ref, dg0_ref, du0_ref, dg1_ref, du1_ref, *refs):
        og_ref, ou_ref = refs[-2:]
        for e, (g_ref, u_ref) in enumerate(((dg0_ref, du0_ref), (dg1_ref, du1_ref))):
            @pl.when(pl.program_id(0) == e)
            def _(g_ref=g_ref, u_ref=u_ref):
                og_ref[...] = dot(x_ref[...], g_ref[...], 0, 0).astype(BF16)
                ou_ref[...] = dot(x_ref[...], u_ref[...], 0, 0).astype(BF16)

    whole = pl.BlockSpec((slots, units), lambda e, k, s: (0, 0))
    made = pl.BlockSpec((None, tile, units), lambda e, k, s: (e, k, 0))
    return call(
        kernel,
        where,
        (experts, cols // tile),
        [pl.BlockSpec((None, slots, tile), lambda e, k, s: (e, 0, k))] + [whole] * 4 + unused(after),
        [made, made],
        [out((experts, cols, units), BF16)] * 2,
        (saved_input, dg0, du0, dg1, du1, *after),
    )


def body(grad_out, routes, loss_weight, saved_input, saved_gate, saved_up, w_gate, w_up, w_down):
    groups = lax.axis_size("dp")
    splits = lax.axis_size("expert")
    pos = lax.axis_index("expert")
    my_x, my_c = pos // CORES, pos % CORES
    where = jnp.stack([my_x, my_c]).astype(jnp.int32)
    experts = w_gate.shape[0]
    tokens = grad_out.shape[0]
    width = grad_out.shape[1]
    cols = width // splits
    slots = saved_input.shape[1]
    cap = slots // (groups * splits)
    lanes = saved_gate.shape[2]

    chosen = routes.reshape(-1)
    order = jnp.arange(chosen.shape[0], dtype=jnp.int32)
    same = (chosen[:, None] == chosen[None, :]) & (order[:, None] < order[None, :])
    rank = jnp.sum(same.astype(jnp.int32), axis=0)
    row = (chosen % experts) * slots + (chosen // experts) * (splits * cap) + pos * cap + rank
    row = row.reshape(tokens, 2).T
    code = jnp.concatenate([row // 64, row % 64], axis=0).astype(BF16)
    code = jnp.pad(code, ((0, 4), (0, cols - tokens)))
    code = jnp.concatenate([code, code], axis=1)

    scaled = (grad_out.astype(F32) * loss_weight.astype(F32)[:, None] * 0.25).astype(BF16)
    near, far = [], []
    for dx in range(X_CHIPS):
        piece = lax.dynamic_slice(
            scaled, (0, (my_x + dx) % X_CHIPS * (CORES * cols)), (tokens, CORES * cols)
        )
        piece = jnp.concatenate([piece, code], axis=0)
        if dx:
            piece = along_x(piece, dx)
        near.append(lax.dynamic_slice(piece, (0, my_c * cols), (tokens + 8, cols)))
        far.append(swap_core(lax.dynamic_slice(piece, (0, (1 - my_c) * cols), (tokens + 8, cols))))
    gathered = jnp.stack(near + far)
    codes = gathered[:, tokens : tokens + 4, :tokens].astype(jnp.int32)
    row_of = (codes[:, :2] * 64 + codes[:, 2:]).transpose(1, 0, 2).reshape(2, splits * tokens)
    gathered = gathered[:, :tokens].reshape(splits * tokens, cols)

    index = jnp.arange(slots, dtype=jnp.int32)[:, None]
    placed = [
        ((row_of[0][None, :] == index + e * slots) | (row_of[1][None, :] == index + e * slots)).astype(BF16)
        for e in range(experts)
    ]
    outgoing = [dot(placed[e], gathered, 1, 0).astype(BF16) for e in range(experts)]
    dispatched = [
        lax.all_to_all(
            o.reshape(groups, splits * cap, cols), "dp", split_axis=0, concat_axis=0, tiled=True
        ).reshape(slots, cols)
        for o in outgoing
    ]

    both = both_saved(
        where,
        saved_gate.reshape(experts * slots, lanes),
        saved_up.reshape(experts * slots, lanes),
        (gathered,),
    )
    ahead, behind = along_x(both, 1), along_x(both, 3)
    pick_a, pick_b = forwarded(where, ahead, behind, ())
    across = (along_x(pick_a, 1), along_x(pick_b, 3))
    held = [(both, both), (ahead, ahead), across, (behind, behind)]
    both_o, ahead_o, behind_o = swap_core(both), swap_core(ahead), swap_core(behind)
    across_o = (swap_core(across[0]), swap_core(across[1]))
    held += [(both_o, both_o), (ahead_o, ahead_o), across_o, (behind_o, behind_o)]

    def partials(e, after, after_pair):
        keep, give = hidden_partials(where, e, dispatched[e], w_down, after)
        return pair_sums(where, keep, swap_core(give), after_pair)

    def exchanged(sent):
        return [along_x(v, dx) for dx, v in enumerate(sent, 1)]

    def spread(own):
        pieces = [own] + [along_x(own, dx) for dx in range(1, X_CHIPS)]
        return pieces + [swap_core(v) for v in pieces]

    def give_back(slot_grad):
        returned = lax.all_to_all(
            slot_grad.reshape(groups, splits * cap, cols), "dp", split_axis=0, concat_axis=0, tiled=True
        )
        return returned.reshape(slots, cols)

    first0, *sent0 = partials(0, (both_o, ahead_o, behind_o, *across), ())
    own0 = chip_sums(where, first0, exchanged(sent0), across_o)
    pieces0 = spread(own0)
    first1, *sent1 = partials(1, (own0,), ())
    own1 = chip_sums(where, first1, exchanged(sent1), ())
    dgate0, dup0, hidden0, slot_grad0 = slot_gradient(where, 0, pieces0, held, w_gate, w_up, (own1,))
    returned0 = give_back(slot_grad0)
    pieces1 = spread(own1)
    dgate1, dup1, hidden1, slot_grad1 = slot_gradient(where, 1, pieces1, held, w_gate, w_up, ())
    returned1 = give_back(slot_grad1)
    back0 = dot(placed[0], returned0, 0, 0)
    grad_down = down_gradient(where, hidden0, hidden1, *dispatched)
    grad_gate, grad_up = up_gradients(where, saved_input, dgate0, dup0, dgate1, dup1, (back0,))
    returned1, grad_down, grad_gate, grad_up = lax.optimization_barrier(
        (returned1, grad_down, grad_gate, grad_up)
    )
    half = X_CHIPS * tokens

    def joined(low):
        here = slice(low, low + half)
        total = back0[here] + dot(placed[1][:, here], returned1, 0, 0)
        return total.astype(BF16).reshape(X_CHIPS, tokens, cols)

    other = swap_core(joined(half))
    mine = joined(0)
    grad_input = jnp.zeros((tokens, width), BF16)
    for dx in range(X_CHIPS):
        for core, v in ((my_c, mine), (1 - my_c, other)):
            piece = along_x(v[dx], X_CHIPS - dx) if dx else v[dx]
            at = ((my_x + dx) % X_CHIPS * CORES + core) * cols
            grad_input = lax.dynamic_update_slice(grad_input, piece, (0, at))
    return (grad_input, grad_gate, grad_up, grad_down)


def solution(mesh):
    return jax.shard_map(
        body,
        mesh=mesh,
        in_specs=(
            P(("dp", "expert"), None),
            P(("dp", "expert"), None),
            P(("dp", "expert")),
            P("dp", None, "expert"),
            P("dp", None, "expert"),
            P("dp", None, "expert"),
            P("dp", "expert", None),
            P("dp", "expert", None),
            P("dp", None, "expert"),
        ),
        out_specs=(
            P(("dp", "expert"), None),
            P("dp", "expert", None),
            P("dp", "expert", None),
            P("dp", None, "expert"),
        ),
        check_vma=False,
    )
```
